1024 devices in a mesh: gx: 16 (over z), gy: 4 (over y_hi), gz: 16 (over x, y_lo, core).
Axes of the slice: x: 4, y: 8 (y_hi: 4, y_lo: 2; y = y_hi * 2 + y_lo), z: 16, core: 2. Of those that a mesh axis runs over, the one named last changes fastest.
Arguments:
- orbitals: float32 [2, 256, 64, 2048], P(None, 'gx', 'gy', 'gz'), may hold values from -6 to 6
- potential: float32 [256, 64, 2048], P('gx', 'gy', 'gz'), may hold values from -2 to 1
- projectors: float32 [16, 4, 16, 8, 4, 4, 4096], P('gx', 'gy', 'gz'), as said below
- coupling: float32 [16, 4, 16, 8, 4, 4, 4], P('gx', 'gy', 'gz'), as said below
- block_starts: int32 [16, 4, 16, 8, 4, 3], P('gx', 'gy', 'gz'), may hold values from 0 to 127, as said below
- owner_counts: int32 [16, 4, 16, 8], P('gx', 'gy', 'gz'), may hold values from 1 to 4, as said below
Outputs:
- applied: float32 [2, 256, 64, 2048], P(None, 'gx', 'gy', 'gz')
The draws below stay inside these ranges and needn't reach their ends.
Inputs may be any that keep to these rules, and one draw needn't show every extreme that they name: `block_starts`: entry [q, o, s, d] is the start along dimension d, inside its owner box, of the block of slot s of the box q - o (periodically, o = (a, b, c) with c fastest); it is below 16, 16, 128 for d = 0, 1, 2, and all eight copies of an atom agree. `owner_counts`: entry [q, o] is the number of live slots of the box q - o (periodically, o ordered as in block_starts); the eight copies agree. `projectors`: the eight copies of an atom's values agree. `coupling`: the eight copies of an atom's matrix agree.
All inputs are finite; a program needn't handle non-finite values.
Results may differ from the reference program's by a relative error of at most 0.00005.
Values sent between devices are 32-bit elements; how exact they have to be, the bound alone decides.
No kernel may reach another device: no remote copies, remote signals or barrier semaphores. Data moves between devices by JAX's collectives and lax.ppermute only.
A program may use at most 64 MiB of HBM per device.

```python
import jax
import jax.numpy as jnp
from jax import lax

CX = 16
CY = 16
CZ = 128
BANDS = 2
PB = 16
NPROJ = 4
SLOTS = 4
NX = 256
NY = 64
NZ = 2048
N_GX = 16
N_GY = 4
N_GZ = 16


def spread(owner):
    copies = []
    for shift_a in (0, 1):
        for shift_b in (0, 1):
            for shift_c in (0, 1):
                copies.append(jnp.roll(owner, (shift_a, shift_b, shift_c), axis=(0, 1, 2)))
    return jnp.stack(copies, axis=3)


def draw_block_starts(key, part):
    key = jax.random.fold_in(key, 11)
    keys = jax.random.split(key, 3)
    shape = (N_GX, N_GY, N_GZ, SLOTS)
    start_x = jax.random.randint(keys[0], shape, 0, CX)
    start_y = jax.random.randint(keys[1], shape, 0, CY)
    start_z = jax.random.randint(keys[2], shape, 0, CZ)
    owner = jnp.stack([start_x, start_y, start_z], axis=-1).astype(jnp.int32)
    owner = owner.at[0, 0, 0, 0].set(jnp.array([CX - 1, CY - 1, CZ - 1], jnp.int32))
    owner = owner.at[0, 0, 0, 1].set(jnp.zeros((3,), jnp.int32))
    return spread(owner)


def draw_owner_counts(key, part):
    key = jax.random.fold_in(key, 17)
    owner = jax.random.randint(key, (N_GX, N_GY, N_GZ), 1, SLOTS + 1).astype(jnp.int32)
    owner = owner.at[0, 0, 0].set(SLOTS)
    return spread(owner)


def draw_projectors(key, part):
    key = jax.random.fold_in(key, 23)
    keys = jax.random.split(key, 1)
    shape = (N_GX, N_GY, N_GZ, SLOTS, NPROJ, PB ** 3)
    owner = jax.random.normal(keys[0], shape, jnp.float32) * 0.125
    return spread(owner)


def draw_coupling(key, part):
    key = jax.random.fold_in(key, 31)
    keys = jax.random.split(key, 2)
    shape = (N_GX, N_GY, N_GZ, SLOTS, NPROJ, NPROJ)
    diag = jax.random.uniform(keys[0], shape[:5], jnp.float32, 0.5, 2.0)
    off = jax.random.normal(keys[1], shape, jnp.float32) * 0.25
    off = 0.5 * (off + jnp.swapaxes(off, -1, -2))
    unit = jnp.eye(NPROJ, dtype=jnp.float32)
    owner = off * (1.0 - unit) + diag[..., None] * unit
    return spread(owner)


def block_scale(own_key, dims, cuts, least, largest):
    def one(axis_at, shards_of):
        steps = jax.random.uniform(jax.random.fold_in(jax.random.fold_in(own_key, 6), axis_at), (shards_of,), jnp.float32, least / len(cuts), largest / len(cuts))
        return jnp.repeat(jnp.exp(steps), dims[axis_at] // shards_of).reshape((-1,) + (1,) * (len(dims) - axis_at - 1))

    gain = one(*cuts[0])
    for cut in cuts[1:]:
        gain = gain * one(*cut)
    return gain


def bell_draw(rng, extent, width, most, cuts=(), held_as=jnp.bfloat16):
    drawn = width * jax.random.normal(rng, extent, jnp.float32)
    if cuts:
        drawn = drawn * block_scale(rng, extent, cuts, -0.22, 0.18)
    return jnp.clip(drawn, -most, most).astype(held_as)


def setup_inputs(seed: int = 0) -> dict:
    key_list = jax.random.split(jax.random.key(seed), 7)
    orbitals = bell_draw(key_list[0], (BANDS, NX, NY, NZ), 1.0, 6.0, ((1, 16), (2, 4), (3, 16)), jnp.float32)
    potential = jnp.clip(-2.0 + 3.0 * jax.random.uniform(key_list[1], (NX, NY, NZ), jnp.float32) ** block_scale(key_list[1], (NX, NY, NZ), ((0, 16), (1, 4), (2, 16)), -0.2, 0.2), -2.0, 1.0)
    projectors = draw_projectors(jax.random.fold_in(key_list[6], 71), 0)
    coupling = draw_coupling(jax.random.fold_in(key_list[6], 71), 0)
    block_starts = draw_block_starts(jax.random.fold_in(key_list[6], 71), 0)
    owner_counts = draw_owner_counts(jax.random.fold_in(key_list[6], 71), 0)
    return dict(orbitals=orbitals, potential=potential, projectors=projectors, coupling=coupling, block_starts=block_starts, owner_counts=owner_counts)


COEFF = [-5369.0 / 1800.0, 12.0 / 7.0, -15.0 / 56.0, 10.0 / 189.0, -1.0 / 112.0, 2.0 / 1925.0, -1.0 / 16632.0]


def laplace(field):
    total = 3.0 * COEFF[0] * field
    for axis_id in (1, 2, 3):
        for step in range(1, 7):
            total = total + COEFF[step] * (jnp.roll(field, step, axis_id) + jnp.roll(field, -step, axis_id))
    return total


def reference(orbitals, potential, projectors, coupling, block_starts, owner_counts):
    bands = orbitals.shape[0]
    boxes_x, boxes_y, boxes_z = block_starts.shape[0], block_starts.shape[1], block_starts.shape[2]
    starts = block_starts[:, :, :, 0]
    base_x = (jnp.arange(boxes_x, dtype=jnp.int32) * CX)[:, None, None, None]
    base_y = (jnp.arange(boxes_y, dtype=jnp.int32) * CY)[None, :, None, None]
    base_z = (jnp.arange(boxes_z, dtype=jnp.int32) * CZ)[None, None, :, None]
    glob_x = (base_x + starts[..., 0]).reshape(-1)
    glob_y = (base_y + starts[..., 1]).reshape(-1)
    glob_z = (base_z + starts[..., 2]).reshape(-1)
    span = jnp.arange(PB, dtype=jnp.int32)
    index_x = ((glob_x[:, None] + span[None, :]) % NX)[:, :, None, None]
    index_y = ((glob_y[:, None] + span[None, :]) % NY)[:, None, :, None]
    index_z = ((glob_z[:, None] + span[None, :]) % NZ)[:, None, None, :]
    blocks = orbitals[:, index_x, index_y, index_z].reshape(bands, -1, PB ** 3)
    values = projectors[:, :, :, 0].reshape(-1, NPROJ, PB ** 3)
    coefficients = jnp.einsum('bkc,kjc->kbj', blocks, values, precision=lax.Precision.HIGHEST)
    slot_ids = jnp.arange(SLOTS, dtype=jnp.int32)
    live = (slot_ids[None, :] < owner_counts[:, :, :, 0].reshape(-1, 1)).astype(jnp.float32).reshape(-1)
    matrices = coupling[:, :, :, 0].reshape(-1, NPROJ, NPROJ)
    weighted = jnp.einsum('kij,kbj->kbi', matrices, coefficients, precision=lax.Precision.HIGHEST) * live[:, None, None]
    contrib = jnp.einsum('kbj,kjc->bkc', weighted, values, precision=lax.Precision.HIGHEST)
    contrib = contrib.reshape(bands, -1, PB, PB, PB)
    nonlocal_part = jnp.zeros_like(orbitals).at[:, index_x, index_y, index_z].add(contrib)
    return -0.5 * laplace(orbitals) + potential[None] * orbitals + nonlocal_part
```

```python
import jax
import jax.numpy as jnp
from jax import lax
from jax.experimental import pallas as pl
from jax.experimental.pallas import tpu as pltpu
from jax.sharding import PartitionSpec as P

PB = 16
NPROJ = 4
SLOTS = 4
BANDS = 2
CX = 16
CY = 16
CZ = 128
RADIUS = 6
EDGE = BANDS * RADIUS * CX
MiB = 1 << 20

COEFF = [
    -5369.0 / 1800.0,
    12.0 / 7.0,
    -15.0 / 56.0,
    10.0 / 189.0,
    -1.0 / 112.0,
    2.0 / 1925.0,
    -1.0 / 16632.0,
]
HALF = [-0.5 * c for c in COEFF]
HI = lax.Precision.HIGHEST
F32 = jnp.float32

VM = pl.BlockSpec(memory_space=pltpu.VMEM)
SM = pl.BlockSpec(memory_space=pltpu.SMEM)


def params():
    return pltpu.CompilerParams(vmem_limit_bytes=24 * MiB)


def iota(shape, dim):
    return lax.broadcasted_iota(jnp.int32, shape, dim)


def contract(a, b, dims):
    return lax.dot_general(a, b, (dims, ((), ())), precision=HI, preferred_element_type=F32)


def place(starts, counts, k):
    o = k >> 2
    s = k & 3
    lx = starts[0, 0, 0, o, s, 0] - CX * (o >> 2)
    ly = starts[0, 0, 0, o, s, 1] - CY * ((o >> 1) & 1)
    lz = starts[0, 0, 0, o, s, 2] - CZ * (o & 1)
    live = (s < counts[0, 0, 0, o]) & (lx > -PB) & (ly > -PB) & (lz > -PB)
    return lx, ly, lz, live


def z_inside(lz):
    z = (iota((8, 128), 1) & 15) + lz
    return (z >= 0) & (z < CZ)


def line_of(y):
    return jnp.where((y >= 0) & (y < CY), y, CY)


def splat(row):
    return jnp.broadcast_to(row, (8, 128))


def gather_kernel(starts, counts, x, proj, up_x, dn_x, up_y, dn_y, zed, part, turned, sums, rows):
    flat = x.reshape(BANDS * CX * CY, 128)
    zero = jnp.zeros((16, 128), F32)
    for b in range(BANDS):
        for y in range(CY):
            turned[b, y, 0:16, :] = zero
            turned[b, y, 32:48, :] = zero
            for h in range(2):
                turned[b, y, 16 + 8 * h : 24 + 8 * h, :] = flat[
                    pl.ds(256 * b + 128 * h + y, 8, stride=16), :
                ]
        turned[b, CY, :, :] = jnp.zeros((48, 128), F32)
    rows[...] = jnp.zeros_like(rows)
    group = iota((8, 128), 1) >> 4

    def atom(k, _):
        lx, ly, lz, live = place(starts, counts, k)

        @pl.when(live)
        def _():
            inside = z_inside(lz)
            acc = [None] * 8
            for h in range(2):
                packed = {}
                for r in range(8):
                    turn = (16 * r - lz + 128) & 127
                    y = line_of(ly + 8 * h + r)
                    for b in range(BANDS):
                        for q in range(2):
                            v = turned[b, y, pl.ds(lx + 16 + 8 * q, 8), :]
                            v = pltpu.roll(v, turn, 1)
                            packed[b, q] = v if r == 0 else jnp.where(group == r, v, packed[b, q])
                for q in range(2):
                    cells = [jnp.where(inside, packed[b, q], 0.0) for b in range(BANDS)]
                    for j in range(NPROJ):
                        p = proj[k, pl.ds(64 * q + 4 * h + j, 8, stride=8), :]
                        for b in range(BANDS):
                            n = b * NPROJ + j
                            t = cells[b] * p
                            acc[n] = t if acc[n] is None else acc[n] + t
            for n in range(8):
                sums[8 * n : 8 * n + 8, :] = acc[n]
            total = sums[pl.ds(0, 8, stride=8), :]
            for n in range(1, 8):
                total = total + sums[pl.ds(n, 8, stride=8), :]
            rows[pl.ds(pl.multiple_of(k * 8, 8), 8), :] = total

        return 0

    lax.fori_loop(0, 8 * SLOTS, atom, 0)
    coef = contract(jnp.ones((8, 128), F32), rows[...], ((1,), (1,)))
    part[0:8, :] = coef[:, 0:128]
    part[8:16, :] = coef[:, 128:256]
    for b in range(BANDS):
        up_x[96 * b : 96 * b + 96, :] = x[b, 10:16].reshape(96, 128)
        dn_x[96 * b : 96 * b + 96, :] = x[b, 0:6].reshape(96, 128)
    up_x[192:200, :] = coef[:, 0:128]
    dn_x[192:200, :] = coef[:, 128:256]
    for b in range(BANDS):
        for i in range(CX):
            at = (b * CX + i) * RADIUS
            up_y[at : at + RADIUS, :] = x[b, i, 10:16, :]
            dn_y[at : at + RADIUS, :] = x[b, i, 0:6, :]
    row, lane = iota((16, 128), 0), iota((16, 128), 1)
    pick_up = (row < 6) & (lane == row + 122)
    pick_dn = (row >= 8) & (row < 14) & (lane == row - 8)
    pick = jnp.where(pick_up | pick_dn, 1.0, 0.0).astype(F32)
    flat = x[...].reshape(BANDS * CX * CY, 128)
    zed[...] = contract(pick, flat, ((1,), (1,)))


def local_kernel(x, pot, out):
    row, lane = iota((128, 128), 0), iota((128, 128), 1)
    far = jnp.abs(row - lane)
    band = jnp.where(far == 0, 3.0 * HALF[0], 0.0)
    for k in range(1, 7):
        band = jnp.where(far == k, HALF[k], band)
    flat = x[...].reshape(BANDS * CX * CY, 128)
    out[...] = contract(flat, band.astype(F32), ((1,), (0,))).reshape(BANDS, CX, CY, CZ)
    for b in range(BANDS):
        out[b] = out[b] + pot[...] * x[b]


def x_kernel(x, low, high, acc, out):
    for b in range(BANDS):

        def plane(i, b=b):
            if i < 0:
                at = 96 * b + 16 * (i + 6)
                return low[at : at + 16, :]
            if i >= CX:
                at = 96 * b + 16 * (i - CX)
                return high[at : at + 16, :]
            return x[b, i]

        for i in range(CX):
            total = acc[b, i]
            for k in range(1, 7):
                total = total + HALF[k] * (plane(i + k) + plane(i - k))
            out[b, i] = total


def y_kernel(x, low, high, acc, out, wide):
    for b in range(BANDS):
        for i in range(CX):
            at = (b * CX + i) * RADIUS
            wide[b, i, 2:8, :] = low[at : at + RADIUS, :]
            wide[b, i, 8:24, :] = x[b, i]
            wide[b, i, 24:30, :] = high[at : at + RADIUS, :]

    for b in range(BANDS):

        def line(i, _, b=b):
            total = acc[b, i]
            for k in range(1, 7):
                total = total + HALF[k] * (
                    wide[b, i, 8 + k : 24 + k, :] + wide[b, i, 8 - k : 24 - k, :]
                )
            out[b, i] = total
            return 0

        lax.fori_loop(0, CX, line, 0, unroll=4)


def spread_kernel(starts, counts, coupling, proj, sums, z_lo, z_hi, acc, out, turned, coef):
    eye = iota((128, 128), 0) == iota((128, 128), 1)
    ones = jnp.ones((128, 128), F32)
    for a in range(2):
        row = jnp.broadcast_to(sums[8 * a : 8 * a + 1, :], (128, 128))
        coef[128 * a : 128 * a + 128, :] = contract(jnp.where(eye, row, 0.0), ones, ((1,), (0,)))
    turned[...] = jnp.zeros_like(turned)
    group = iota((8, 128), 1) >> 4

    def atom(k, _):
        lx, ly, lz, live = place(starts, counts, k)

        @pl.when(live)
        def _():
            inside = z_inside(lz)
            own = coef[pl.ds(pl.multiple_of(k * 8, 8), 8), :]
            weight = []
            for b in range(BANDS):
                c = [splat(own[b * NPROJ + j : b * NPROJ + j + 1, :]) for j in range(NPROJ)]
                for i in range(NPROJ):
                    total = coupling[0, 0, 0, k >> 2, k & 3, i, 0] * c[0]
                    for j in range(1, NPROJ):
                        total = total + coupling[0, 0, 0, k >> 2, k & 3, i, j] * c[j]
                    weight.append(total)
            for h in range(2):
                packed = {}
                for q in range(2):
                    p = [
                        proj[k, pl.ds(64 * q + 4 * h + j, 8, stride=8), :] for j in range(NPROJ)
                    ]
                    for b in range(BANDS):
                        v = weight[b * NPROJ] * p[0]
                        for j in range(1, NPROJ):
                            v = v + weight[b * NPROJ + j] * p[j]
                        packed[b, q] = jnp.where(inside, v, 0.0)
                for r in range(8):
                    turn = (lz - 16 * r + 256) & 127
                    y = line_of(ly + 8 * h + r)
                    for b in range(BANDS):
                        for q in range(2):
                            v = jnp.where(group == r, packed[b, q], 0.0)
                            v = pltpu.roll(v, turn, 1)
                            at = pl.ds(lx + 16 + 8 * q, 8)
                            turned[b, y, at, :] = turned[b, y, at, :] + v

        return 0

    lax.fori_loop(0, 8 * SLOTS, atom, 0)
    edge = jnp.concatenate([z_lo[...], z_hi[...]], axis=0)
    row, lane = iota((16, 128), 0), iota((16, 128), 1)
    low = row < 8
    far = jnp.where(low, lane + 6 - row, 128 + (row - 8) - lane)
    real = (row & 7) < 6
    tail = jnp.zeros((16, 128), F32)
    for k in range(1, 7):
        tail = jnp.where(real & (far == k), HALF[k], tail)
    z_part = contract(edge, tail, ((0,), (0,))).reshape(BANDS, CX, CY, CZ)
    flat = turned.reshape(BANDS * (CY + 1) * 48, 128)
    for b in range(BANDS):
        for i in range(CX):
            for h in range(2):
                first = (b * (CY + 1) + 8 * h) * 48 + 16 + i
                at = slice(8 * h, 8 * h + 8)
                spread = flat[pl.ds(first, 8, stride=48), :]
                out[b, i, at, :] = acc[b, i, at, :] + z_part[b, i, at, :] + spread


def shape(*dims):
    return jax.ShapeDtypeStruct(dims, F32)


def shifted(value, axis, distance):
    n = lax.axis_size(axis)
    return lax.ppermute(value, axis, [(i, (i + distance) % n) for i in range(n)])


def on_device(orbitals, potential, projectors, coupling, block_starts, owner_counts):
    grid = shape(BANDS, CX, CY, CZ)
    projectors = projectors.reshape(8, SLOTS, NPROJ, 32, 128).transpose(0, 1, 3, 2, 4)
    projectors = projectors.reshape(8 * SLOTS, 32 * NPROJ, 128)
    up_x, dn_x, up_y, dn_y, zed, part = pl.pallas_call(
        gather_kernel,
        out_shape=[
            shape(EDGE + 8, 128),
            shape(EDGE + 8, 128),
            shape(EDGE, 128),
            shape(EDGE, 128),
            shape(16, 512),
            shape(16, 128),
        ],
        in_specs=[SM, SM, VM, VM],
        out_specs=[VM] * 6,
        scratch_shapes=[
            pltpu.VMEM((BANDS, CY + 1, 48, 128), F32),
            pltpu.VMEM((64, 128), F32),
            pltpu.VMEM((256, 128), F32),
        ],
        compiler_params=params(),
        name="gather",
    )(block_starts, owner_counts, orbitals, projectors)

    from_low = shifted(up_x, "gx", 1)
    from_high = shifted(dn_x, "gx", -1)
    acc = pl.pallas_call(
        local_kernel,
        out_shape=grid,
        in_specs=[VM] * 2,
        out_specs=VM,
        compiler_params=params(),
        name="local",
    )(orbitals, potential)
    x_low, x_high = from_low[:EDGE], from_high[:EDGE]
    sums = part + jnp.concatenate([from_high[EDGE:], from_low[EDGE:]], axis=0)

    from_low = shifted(jnp.concatenate([up_y, sums], axis=0), "gy", 1)
    from_high = shifted(jnp.concatenate([dn_y, sums], axis=0), "gy", -1)
    acc = pl.pallas_call(
        x_kernel,
        out_shape=grid,
        in_specs=[VM] * 4,
        out_specs=VM,
        compiler_params=params(),
        name="along_x",
    )(orbitals, x_low, x_high, acc)
    y_low, y_high = from_low[:EDGE], from_high[:EDGE]
    lane = iota((16, 128), 1)
    first = (lane & 64) == 0
    sums = sums + jnp.where(
        first, jnp.roll(from_high[EDGE:], -64, 1), jnp.roll(from_low[EDGE:], 64, 1)
    )

    flat = sums.reshape(2, 8, 128).transpose(1, 0, 2).reshape(8, 256)
    from_low = shifted(jnp.concatenate([zed[0:8], flat], axis=1), "gz", 1)
    from_high = shifted(jnp.concatenate([zed[8:16], flat], axis=1), "gz", -1)
    acc = pl.pallas_call(
        y_kernel,
        out_shape=grid,
        in_specs=[VM] * 4,
        out_specs=VM,
        scratch_shapes=[pltpu.VMEM((BANDS, CX, 32, 128), F32)],
        compiler_params=params(),
        name="along_y",
    )(orbitals, y_low, y_high, acc)
    lane = iota((8, 256), 1)
    first = (lane & 32) == 0
    flat = flat + jnp.where(
        first, jnp.roll(from_high[:, 512:], -32, 1), jnp.roll(from_low[:, 512:], 32, 1)
    )
    sums = flat.reshape(8, 2, 128).transpose(1, 0, 2).reshape(16, 128)
    return pl.pallas_call(
        spread_kernel,
        out_shape=grid,
        in_specs=[SM, SM, SM] + [VM] * 5,
        out_specs=VM,
        scratch_shapes=[
            pltpu.VMEM((BANDS, CY + 1, 48, 128), F32),
            pltpu.VMEM((256, 128), F32),
        ],
        compiler_params=params(),
        name="spread",
    )(
        block_starts,
        owner_counts,
        coupling,
        projectors,
        sums,
        from_low[:, :512],
        from_high[:, :512],
        acc,
    )


def solution(mesh):
    in_specs = (
        P(None, "gx", "gy", "gz"),
        P("gx", "gy", "gz"),
        P("gx", "gy", "gz", None, None, None, None),
        P("gx", "gy", "gz", None, None, None, None),
        P("gx", "gy", "gz", None, None, None),
        P("gx", "gy", "gz", None),
    )
    out_specs = P(None, "gx", "gy", "gz")
    return jax.shard_map(
        on_device, mesh=mesh, in_specs=in_specs, out_specs=out_specs, check_vma=False
    )
```

```python
import jax
import jax.numpy as jnp
from jax import lax
from jax.experimental import pallas as pl
from jax.experimental.pallas import tpu as pltpu
from jax.sharding import PartitionSpec as P

PB = 16
NPROJ = 4
SLOTS = 4
BANDS = 2
CX = 16
CY = 16
CZ = 128
RADIUS = 6
EDGE = BANDS * RADIUS * CX
MiB = 1 << 20

COEFF = [
    -5369.0 / 1800.0,
    12.0 / 7.0,
    -15.0 / 56.0,
    10.0 / 189.0,
    -1.0 / 112.0,
    2.0 / 1925.0,
    -1.0 / 16632.0,
]
HALF = [-0.5 * c for c in COEFF]
HI = lax.Precision.HIGHEST
F32 = jnp.float32

VM = pl.BlockSpec(memory_space=pltpu.VMEM)
HB = pl.BlockSpec(memory_space=pl.ANY)
PLACES = [
    pltpu.SMEM((1, 1, 1, 3, SLOTS, 8), jnp.int32),
    pltpu.SMEM((1, 1, 1, 8), jnp.int32),
]
MATRICES = [pltpu.SMEM((1, 1, 1, SLOTS, NPROJ, NPROJ, 8), F32)]
LISTED = [pltpu.SMEM((8 * SLOTS,), jnp.int32), pltpu.SemaphoreType.DMA((3,))]


def params():
    return pltpu.CompilerParams(vmem_limit_bytes=24 * MiB)


def iota(shape, dim):
    return lax.broadcasted_iota(jnp.int32, shape, dim)


def contract(a, b, dims):
    return lax.dot_general(a, b, (dims, ((), ())), precision=HI, preferred_element_type=F32)


def place(starts, counts, k):
    o = k >> 2
    s = k & 3
    lx = starts[0, 0, 0, 0, s, o] - CX * (o >> 2)
    ly = starts[0, 0, 0, 1, s, o] - CY * ((o >> 1) & 1)
    lz = starts[0, 0, 0, 2, s, o] - CZ * (o & 1)
    live = (s < counts[0, 0, 0, o]) & (lx > -PB) & (ly > -PB) & (lz > -PB)
    whole = (lz >= 0) & (lz <= CZ - PB)
    return lx, ly, lz, live, whole


def begin(pairs, sems):
    copies = [pltpu.make_async_copy(a, b, sems.at[n]) for n, (a, b) in enumerate(pairs)]
    for copy in copies:
        copy.start()
    return copies


def chosen(starts, counts, which, listed):
    n = jnp.int32(0)
    for k in range(8 * SLOTS):
        _, _, _, live, whole = place(starts, counts, k)
        listed[n] = k
        n = n + which(live, whole).astype(jnp.int32)
    return n


def line_of(y):
    return jnp.where((y >= 0) & (y < CY), y, CY)


def splat(row):
    return jnp.broadcast_to(row, (8, 128))


def turn_about(source, target):
    flat = source.reshape(BANDS * CX * CY, 128)
    zero = jnp.zeros((16, 128), F32)
    for b in range(BANDS):
        for y in range(CY):
            target[b, y, 0:16, :] = zero
            target[b, y, 32:48, :] = zero
            for h in range(2):
                target[b, y, 16 + 8 * h : 24 + 8 * h, :] = flat[
                    pl.ds(256 * b + 128 * h + y, 8, stride=16), :
                ]
        target[b, CY, :, :] = jnp.zeros((48, 128), F32)


def turn_kernel(x, same, turned, up_x, dn_x, up_y, dn_y):
    same[...] = x[...]
    turn_about(x, turned)
    for b in range(BANDS):
        up_x[96 * b : 96 * b + 96, :] = x[b, 10:16].reshape(96, 128)
        dn_x[96 * b : 96 * b + 96, :] = x[b, 0:6].reshape(96, 128)
        for i in range(CX):
            at = (b * CX + i) * RADIUS
            up_y[at : at + RADIUS, :] = x[b, i, 10:16, :]
            dn_y[at : at + RADIUS, :] = x[b, i, 0:6, :]


def gather_kernel(
    starts_in, counts_in, turned, proj, part, sums, rows, starts, counts, listed, sems
):
    copies = begin([(starts_in, starts), (counts_in, counts)], sems)
    rows[...] = jnp.zeros_like(rows)
    for copy in copies:
        copy.wait()
    group = iota((8, 128), 1) >> 4
    cell = iota((8, 128), 1) & 15

    def atom(n, _):
        k = listed[n]
        lx, ly, lz, _, _ = place(starts, counts, k)
        inside = (cell + lz >= 0) & (cell + lz < CZ)
        acc = [None] * 8
        for h in range(2):
            packed = {}
            for r in range(8):
                turn = (16 * r - lz + 128) & 127
                y = line_of(ly + 8 * h + r)
                for b in range(BANDS):
                    for q in range(2):
                        v = turned[b, y, pl.ds(lx + 16 + 8 * q, 8), :]
                        v = pltpu.roll(v, turn, 1)
                        packed[b, q] = v if r == 0 else jnp.where(group == r, v, packed[b, q])
            for q in range(2):
                cells = [jnp.where(inside, packed[b, q], 0.0) for b in range(BANDS)]
                for j in range(NPROJ):
                    p = proj[k, pl.ds(64 * q + 4 * h + j, 8, stride=8), :]
                    for b in range(BANDS):
                        m = b * NPROJ + j
                        t = cells[b] * p
                        acc[m] = t if acc[m] is None else acc[m] + t
        for m in range(8):
            sums[8 * m : 8 * m + 8, :] = acc[m]
        total = sums[pl.ds(0, 8, stride=8), :]
        for m in range(1, 8):
            total = total + sums[pl.ds(m, 8, stride=8), :]
        rows[pl.ds(pl.multiple_of(k * 8, 8), 8), :] = total

        return 0

    number = chosen(starts, counts, lambda live, whole: live, listed)
    lax.fori_loop(0, number, atom, 0)
    coef = contract(jnp.ones((8, 128), F32), rows[...], ((1,), (1,)))
    part[0:8, :] = coef[:, 0:128]
    part[8:16, :] = coef[:, 128:256]


def local_kernel(x, pot, out, up_z, dn_z):
    row, lane = iota((128, 128), 0), iota((128, 128), 1)
    near = jnp.abs(row - lane)
    band = jnp.where(near == 0, 3.0 * HALF[0], 0.0)
    for k in range(1, 7):
        band = jnp.where(near == k, HALF[k], band)
    flat = x[...].reshape(BANDS * CX * CY, 128)
    total = contract(flat, band.astype(F32), ((1,), (0,)))
    out[...] = total.reshape(BANDS, CX, CY, CZ)
    for b in range(BANDS):
        out[b] = out[b] + pot[...] * x[b]
    row, lane = iota((16, 128), 0), iota((16, 128), 1)
    pick_up = (row < 6) & (lane == row + 122)
    pick_dn = (row >= 8) & (row < 14) & (lane == row - 8)
    pick = jnp.where(pick_up | pick_dn, 1.0, 0.0).astype(F32)
    faces = contract(pick, flat, ((1,), (1,)))
    up_z[...] = faces[0:8]
    dn_z[...] = faces[8:16]


def x_kernel(x, low, high, acc, out):
    for b in range(BANDS):

        def plane(i, b=b):
            if i < 0:
                at = 96 * b + 16 * (i + 6)
                return low[at : at + 16, :]
            if i >= CX:
                at = 96 * b + 16 * (i - CX)
                return high[at : at + 16, :]
            return x[b, i]

        for i in range(CX):
            total = acc[b, i]
            for k in range(1, 7):
                total = total + HALF[k] * (plane(i + k) + plane(i - k))
            out[b, i] = total


def y_kernel(x, low, high, acc, out, wide):
    for b in range(BANDS):
        for i in range(CX):
            at = (b * CX + i) * RADIUS
            wide[b, i, 2:8, :] = low[at : at + RADIUS, :]
            wide[b, i, 8:24, :] = x[b, i]
            wide[b, i, 24:30, :] = high[at : at + RADIUS, :]

    for b in range(BANDS):

        def line(i, _, b=b):
            total = acc[b, i]
            for k in range(1, 7):
                total = total + HALF[k] * (
                    wide[b, i, 8 + k : 24 + k, :] + wide[b, i, 8 - k : 24 - k, :]
                )
            out[b, i] = total
            return 0

        lax.fori_loop(0, CX, line, 0, unroll=4)


def spread(cut, copies, tables, listed, proj, sums, turned, coef):
    starts, counts, coupling = tables
    eye = iota((128, 128), 0) == iota((128, 128), 1)
    ones = jnp.ones((128, 128), F32)
    for a in range(2):
        row = jnp.broadcast_to(sums[8 * a : 8 * a + 1, :], (128, 128))
        coef[128 * a : 128 * a + 128, :] = contract(jnp.where(eye, row, 0.0), ones, ((1,), (0,)))
    turned[...] = jnp.zeros_like(turned)
    group = iota((8, 128), 1) >> 4
    cell = iota((8, 128), 1) & 15

    for copy in copies:
        copy.wait()

    def atom(n, _):
        k = listed[n]
        lx, ly, lz, _, _ = place(starts, counts, k)
        inside = (cell + lz >= 0) & (cell + lz < CZ)
        own = coef[pl.ds(pl.multiple_of(k * 8, 8), 8), :]
        weight = []
        for b in range(BANDS):
            c = [splat(own[b * NPROJ + j : b * NPROJ + j + 1, :]) for j in range(NPROJ)]
            for i in range(NPROJ):
                total = coupling[0, 0, 0, k & 3, i, 0, k >> 2] * c[0]
                for j in range(1, NPROJ):
                    total = total + coupling[0, 0, 0, k & 3, i, j, k >> 2] * c[j]
                weight.append(total)
        for h in range(2):
            packed = {}
            for q in range(2):
                p = [
                    proj[k, pl.ds(64 * q + 4 * h + j, 8, stride=8), :] for j in range(NPROJ)
                ]
                for b in range(BANDS):
                    v = weight[b * NPROJ] * p[0]
                    for j in range(1, NPROJ):
                        v = v + weight[b * NPROJ + j] * p[j]
                    packed[b, q] = jnp.where(inside, v, 0.0)
            for half in range(2):
                batch = []
                for r in range(4 * half, 4 * half + 4):
                    turn = (lz - 16 * r + 256) & 127
                    y = line_of(ly + 8 * h + r)
                    for b in range(BANDS):
                        for q in range(2):
                            v = jnp.where(group == r, packed[b, q], 0.0)
                            at = pl.ds(lx + 16 + 8 * q, 8)
                            v = turned[b, y, at, :] + pltpu.roll(v, turn, 1)
                            batch.append((b, y, at, v))
                for b, y, at, v in batch:
                    turned[b, y, at, :] = v

        return 0

    if cut:
        number = chosen(starts, counts, lambda live, whole: live & jnp.logical_not(whole), listed)
    else:
        number = chosen(starts, counts, lambda live, whole: live & whole, listed)
    lax.fori_loop(0, number, atom, 0)


def fold(b, i, h, turned):
    flat = turned.reshape(BANDS * (CY + 1) * 48, 128)
    return flat[pl.ds((b * (CY + 1) + 8 * h) * 48 + 16 + i, 8, stride=48), :]


def whole_kernel(
    starts_in, counts_in, coupling_in, proj, sums, acc, out, turned, coef,
    starts, counts, coupling, listed, sems,
):
    tables = (starts, counts, coupling)
    copies = begin(list(zip((starts_in, counts_in, coupling_in), tables)), sems)
    spread(False, copies, tables, listed, proj, sums, turned, coef)
    for b in range(BANDS):
        for i in range(CX):
            for h in range(2):
                at = slice(8 * h, 8 * h + 8)
                out[b, i, at, :] = acc[b, i, at, :] + fold(b, i, h, turned)


def cut_kernel(
    starts_in, counts_in, coupling_in, proj, sums, z_low, z_high, acc, out, turned, coef,
    starts, counts, coupling, listed, sems,
):
    tables = (starts, counts, coupling)
    copies = begin(list(zip((starts_in, counts_in, coupling_in), tables)), sems)
    edge = jnp.concatenate([z_low[...], z_high[...]], axis=0)
    row, lane = iota((16, 128), 0), iota((16, 128), 1)
    far = jnp.where(row < 8, lane + 6 - row, 128 + (row - 8) - lane)
    real = (row & 7) < 6
    tail = jnp.zeros((16, 128), F32)
    for k in range(1, 7):
        tail = jnp.where(real & (far == k), HALF[k], tail)
    z_part = contract(edge, tail, ((0,), (0,))).reshape(BANDS, CX, CY, CZ)
    out[...] = acc[...] + z_part
    spread(True, copies, tables, listed, proj, sums, turned, coef)
    for b in range(BANDS):
        for i in range(CX):
            for h in range(2):
                at = slice(8 * h, 8 * h + 8)
                out[b, i, at, :] = out[b, i, at, :] + fold(b, i, h, turned)


def shape(*dims):
    return jax.ShapeDtypeStruct(dims, F32)


def shifted(value, axis, distance):
    n = lax.axis_size(axis)
    return lax.ppermute(value, axis, [(i, (i + distance) % n) for i in range(n)])


def call(kernel, outs, ins, scratch, name, args, flops, bytes_accessed):
    return pl.pallas_call(
        kernel,
        out_shape=outs,
        in_specs=ins,
        out_specs=[VM] * len(outs),
        scratch_shapes=[pltpu.VMEM(s, F32) if isinstance(s, tuple) else s for s in scratch],
        compiler_params=params(),
        cost_estimate=pl.CostEstimate(
            flops=flops, bytes_accessed=bytes_accessed, transcendentals=0
        ),
        name=name,
    )(*args)


def on_device(orbitals, potential, projectors, coupling, block_starts, owner_counts):
    grid = shape(BANDS, CX, CY, CZ)
    padded = (BANDS, CY + 1, 48, 128)
    projectors = projectors.reshape(8, SLOTS, NPROJ, 32, 128).transpose(0, 1, 3, 2, 4)
    projectors = projectors.reshape(8 * SLOTS, 32 * NPROJ, 128)
    starts = block_starts.transpose(0, 1, 2, 5, 4, 3)
    matrices = coupling.transpose(0, 1, 2, 4, 5, 6, 3)

    same, turned, up_x, dn_x, up_y, dn_y = call(
        turn_kernel,
        [grid, shape(*padded)] + [shape(EDGE, 128)] * 4,
        [VM],
        [],
        "turn",
        (orbitals,),
        1 << 30,
        1 << 24,
    )
    (part,) = call(
        gather_kernel,
        [shape(16, 128)],
        [HB, HB, VM, VM],
        [(64, 128), (256, 128)] + PLACES + LISTED,
        "gather",
        (starts, owner_counts, turned, projectors),
        1 << 30,
        1 << 24,
    )

    from_low = shifted(jnp.concatenate([up_x, part[:8]], axis=0), "gx", 1)
    from_high = shifted(jnp.concatenate([dn_x, part[8:]], axis=0), "gx", -1)
    acc, up_z, dn_z = call(
        local_kernel,
        [grid, shape(8, 512), shape(8, 512)],
        [VM] * 2,
        [],
        "local",
        (same, potential),
        1 << 26,
        1 << 20,
    )
    part, acc = lax.optimization_barrier((part, acc))
    x_low, x_high = from_low[:EDGE], from_high[:EDGE]
    sums = part + jnp.concatenate([from_high[EDGE:], from_low[EDGE:]], axis=0)

    from_low = shifted(jnp.concatenate([up_y, sums], axis=0), "gy", 1)
    from_high = shifted(jnp.concatenate([dn_y, sums], axis=0), "gy", -1)
    (acc,) = call(
        x_kernel, [grid], [VM] * 4, [], "along_x", (same, x_low, x_high, acc), 1 << 22, 1 << 20
    )
    sums, acc = lax.optimization_barrier((sums, acc))
    y_low, y_high = from_low[:EDGE], from_high[:EDGE]
    first = (iota((16, 128), 1) & 64) == 0
    sums = sums + jnp.where(
        first, jnp.roll(from_high[EDGE:], -64, 1), jnp.roll(from_low[EDGE:], 64, 1)
    )

    flat = sums.reshape(2, 8, 128).transpose(1, 0, 2).reshape(8, 256)
    from_low = shifted(jnp.concatenate([up_z, flat], axis=1), "gz", 1)
    from_high = shifted(jnp.concatenate([dn_z, flat], axis=1), "gz", -1)
    (acc,) = call(
        y_kernel,
        [grid],
        [VM] * 4,
        [(BANDS, CX, 32, 128)],
        "along_y",
        (same, y_low, y_high, acc),
        1 << 22,
        1 << 20,
    )
    (acc,) = call(
        whole_kernel,
        [grid],
        [HB, HB, HB] + [VM] * 3,
        [padded, (256, 128)] + PLACES + MATRICES + LISTED,
        "whole_blocks",
        (starts, owner_counts, matrices, projectors, sums, acc),
        1 << 30,
        1 << 24,
    )
    first = (iota((8, 256), 1) & 32) == 0
    flat = flat + jnp.where(
        first, jnp.roll(from_high[:, 512:], -32, 1), jnp.roll(from_low[:, 512:], 32, 1)
    )
    sums = flat.reshape(8, 2, 128).transpose(1, 0, 2).reshape(16, 128)
    (out,) = call(
        cut_kernel,
        [grid],
        [HB, HB, HB] + [VM] * 5,
        [padded, (256, 128)] + PLACES + MATRICES + LISTED,
        "cut_blocks",
        (
            starts,
            owner_counts,
            matrices,
            projectors,
            sums,
            from_low[:, :512],
            from_high[:, :512],
            acc,
        ),
        1 << 22,
        1 << 20,
    )
    return out


def solution(mesh):
    in_specs = (
        P(None, "gx", "gy", "gz"),
        P("gx", "gy", "gz"),
        P("gx", "gy", "gz", None, None, None, None),
        P("gx", "gy", "gz", None, None, None, None),
        P("gx", "gy", "gz", None, None, None),
        P("gx", "gy", "gz", None),
    )
    out_specs = P(None, "gx", "gy", "gz")
    return jax.shard_map(
        on_device, mesh=mesh, in_specs=in_specs, out_specs=out_specs, check_vma=False
    )
```

```python
import jax
import jax.numpy as jnp
from jax import lax
from jax.experimental import pallas as pl
from jax.experimental.pallas import tpu as pltpu
from jax.sharding import PartitionSpec as P

PB = 16
NPROJ = 4
SLOTS = 4
BANDS = 2
CX = 16
CY = 16
CZ = 128
RADIUS = 6
EDGE = BANDS * RADIUS * CX
MiB = 1 << 20

COEFF = [
    -5369.0 / 1800.0,
    12.0 / 7.0,
    -15.0 / 56.0,
    10.0 / 189.0,
    -1.0 / 112.0,
    2.0 / 1925.0,
    -1.0 / 16632.0,
]
HALF = [-0.5 * c for c in COEFF]
HI = lax.Precision.HIGHEST
F32 = jnp.float32

VM = pl.BlockSpec(memory_space=pltpu.VMEM)
HB = pl.BlockSpec(memory_space=pl.ANY)
PLACES = [
    pltpu.SMEM((1, 1, 1, 3, SLOTS, 8), jnp.int32),
    pltpu.SMEM((1, 1, 1, 8), jnp.int32),
]
MATRICES = [pltpu.SMEM((1, 1, 1, SLOTS, NPROJ, NPROJ, 8), F32)]
LISTED = [pltpu.SMEM((8 * SLOTS,), jnp.int32), pltpu.SemaphoreType.DMA((3,))]


def params():
    return pltpu.CompilerParams(vmem_limit_bytes=24 * MiB)


def iota(shape, dim):
    return lax.broadcasted_iota(jnp.int32, shape, dim)


def contract(a, b, dims):
    return lax.dot_general(a, b, (dims, ((), ())), precision=HI, preferred_element_type=F32)


def place(starts, counts, k):
    o = k >> 2
    s = k & 3
    lx = starts[0, 0, 0, 0, s, o] - CX * (o >> 2)
    ly = starts[0, 0, 0, 1, s, o] - CY * ((o >> 1) & 1)
    lz = starts[0, 0, 0, 2, s, o] - CZ * (o & 1)
    live = (s < counts[0, 0, 0, o]) & (lx > -PB) & (ly > -PB) & (lz > -PB)
    whole = (lz >= 0) & (lz <= CZ - PB)
    return lx, ly, lz, live, whole


def begin(pairs, sems):
    copies = [pltpu.make_async_copy(a, b, sems.at[n]) for n, (a, b) in enumerate(pairs)]
    for copy in copies:
        copy.start()
    return copies


def chosen(starts, counts, which, listed):
    n = jnp.int32(0)
    for k in range(8 * SLOTS):
        _, _, _, live, whole = place(starts, counts, k)
        listed[n] = k
        n = n + which(live, whole).astype(jnp.int32)
    return n


def line_of(y):
    return jnp.where((y >= 0) & (y < CY), y, CY)


def splat(row):
    return jnp.broadcast_to(row, (8, 128))


def turn_about(source, target):
    flat = source.reshape(BANDS * CX * CY, 128)
    zero = jnp.zeros((16, 128), F32)
    for b in range(BANDS):
        for y in range(CY):
            target[b, y, 0:16, :] = zero
            target[b, y, 32:48, :] = zero
            for h in range(2):
                target[b, y, 16 + 8 * h : 24 + 8 * h, :] = flat[
                    pl.ds(256 * b + 128 * h + y, 8, stride=16), :
                ]
        target[b, CY, :, :] = jnp.zeros((48, 128), F32)


def turn_kernel(x, same, turned, up_x, dn_x, up_y, dn_y):
    same[...] = x[...]
    turn_about(x, turned)
    for b in range(BANDS):
        up_x[96 * b : 96 * b + 96, :] = x[b, 10:16].reshape(96, 128)
        dn_x[96 * b : 96 * b + 96, :] = x[b, 0:6].reshape(96, 128)
        for i in range(CX):
            at = (b * CX + i) * RADIUS
            up_y[at : at + RADIUS, :] = x[b, i, 10:16, :]
            dn_y[at : at + RADIUS, :] = x[b, i, 0:6, :]


def gather_kernel(
    starts_in, counts_in, turned, proj, part, sums, rows, starts, counts, listed, sems
):
    copies = begin([(starts_in, starts), (counts_in, counts)], sems)
    rows[...] = jnp.zeros_like(rows)
    for copy in copies:
        copy.wait()
    group = iota((8, 128), 1) >> 4
    cell = iota((8, 128), 1) & 15

    def atom(n, _):
        k = listed[n]
        lx, ly, lz, _, _ = place(starts, counts, k)
        inside = (cell + lz >= 0) & (cell + lz < CZ)
        acc = [None] * 8
        for h in range(2):
            packed = {}
            for r in range(8):
                turn = (16 * r - lz + 128) & 127
                y = line_of(ly + 8 * h + r)
                for b in range(BANDS):
                    for q in range(2):
                        v = turned[b, y, pl.ds(lx + 16 + 8 * q, 8), :]
                        v = pltpu.roll(v, turn, 1)
                        packed[b, q] = v if r == 0 else jnp.where(group == r, v, packed[b, q])
            for q in range(2):
                cells = [jnp.where(inside, packed[b, q], 0.0) for b in range(BANDS)]
                for j in range(NPROJ):
                    p = proj[k, pl.ds(64 * q + 4 * h + j, 8, stride=8), :]
                    for b in range(BANDS):
                        m = b * NPROJ + j
                        t = cells[b] * p
                        acc[m] = t if acc[m] is None else acc[m] + t
        for m in range(8):
            sums[8 * m : 8 * m + 8, :] = acc[m]
        total = sums[pl.ds(0, 8, stride=8), :]
        for m in range(1, 8):
            total = total + sums[pl.ds(m, 8, stride=8), :]
        rows[pl.ds(pl.multiple_of(k * 8, 8), 8), :] = total

        return 0

    number = chosen(starts, counts, lambda live, whole: live, listed)
    lax.fori_loop(0, number, atom, 0)
    coef = contract(jnp.ones((8, 128), F32), rows[...], ((1,), (1,)))
    part[0:8, :] = coef[:, 0:128]
    part[8:16, :] = coef[:, 128:256]


def local_kernel(x, pot, out, up_z, dn_z):
    row, lane = iota((128, 128), 0), iota((128, 128), 1)
    near = jnp.abs(row - lane)
    band = jnp.where(near == 0, 3.0 * HALF[0], 0.0)
    for k in range(1, 7):
        band = jnp.where(near == k, HALF[k], band)
    flat = x[...].reshape(BANDS * CX * CY, 128)
    total = contract(flat, band.astype(F32), ((1,), (0,)))
    out[...] = total.reshape(BANDS, CX, CY, CZ)
    for b in range(BANDS):
        out[b] = out[b] + pot[...] * x[b]
    row, lane = iota((16, 128), 0), iota((16, 128), 1)
    pick_up = (row < 6) & (lane == row + 122)
    pick_dn = (row >= 8) & (row < 14) & (lane == row - 8)
    pick = jnp.where(pick_up | pick_dn, 1.0, 0.0).astype(F32)
    faces = contract(pick, flat, ((1,), (1,)))
    up_z[...] = faces[0:8]
    dn_z[...] = faces[8:16]


def x_kernel(x, low, high, acc, out):
    for b in range(BANDS):

        def plane(i, b=b):
            if i < 0:
                at = 96 * b + 16 * (i + 6)
                return low[at : at + 16, :]
            if i >= CX:
                at = 96 * b + 16 * (i - CX)
                return high[at : at + 16, :]
            return x[b, i]

        for i in range(CX):
            total = acc[b, i]
            for k in range(1, 7):
                total = total + HALF[k] * (plane(i + k) + plane(i - k))
            out[b, i] = total


def y_kernel(x, low, high, acc, out, wide):
    for b in range(BANDS):
        for i in range(CX):
            at = (b * CX + i) * RADIUS
            wide[b, i, 2:8, :] = low[at : at + RADIUS, :]
            wide[b, i, 8:24, :] = x[b, i]
            wide[b, i, 24:30, :] = high[at : at + RADIUS, :]

    for b in range(BANDS):

        def line(i, _, b=b):
            total = acc[b, i]
            for k in range(1, 7):
                total = total + HALF[k] * (
                    wide[b, i, 8 + k : 24 + k, :] + wide[b, i, 8 - k : 24 - k, :]
                )
            out[b, i] = total
            return 0

        lax.fori_loop(0, CX, line, 0, unroll=4)


def spread(cut, copies, tables, listed, proj, sums, turned, coef):
    starts, counts, coupling = tables
    eye = iota((128, 128), 0) == iota((128, 128), 1)
    ones = jnp.ones((128, 128), F32)
    for a in range(2):
        row = jnp.broadcast_to(sums[8 * a : 8 * a + 1, :], (128, 128))
        coef[128 * a : 128 * a + 128, :] = contract(jnp.where(eye, row, 0.0), ones, ((1,), (0,)))
    turned[...] = jnp.zeros_like(turned)
    group = iota((8, 128), 1) >> 4
    cell = iota((8, 128), 1) & 15

    for copy in copies:
        copy.wait()

    def atom(n, _):
        k = listed[n]
        lx, ly, lz, _, _ = place(starts, counts, k)
        inside = (cell + lz >= 0) & (cell + lz < CZ)
        own = coef[pl.ds(pl.multiple_of(k * 8, 8), 8), :]
        weight = []
        for b in range(BANDS):
            c = [splat(own[b * NPROJ + j : b * NPROJ + j + 1, :]) for j in range(NPROJ)]
            for i in range(NPROJ):
                total = coupling[0, 0, 0, k & 3, i, 0, k >> 2] * c[0]
                for j in range(1, NPROJ):
                    total = total + coupling[0, 0, 0, k & 3, i, j, k >> 2] * c[j]
                weight.append(total)
        for h in range(2):
            packed = {}
            for q in range(2):
                p = [
                    proj[k, pl.ds(64 * q + 4 * h + j, 8, stride=8), :] for j in range(NPROJ)
                ]
                for b in range(BANDS):
                    v = weight[b * NPROJ] * p[0]
                    for j in range(1, NPROJ):
                        v = v + weight[b * NPROJ + j] * p[j]
                    packed[b, q] = jnp.where(inside, v, 0.0)
            for half in range(2):
                batch = []
                for r in range(4 * half, 4 * half + 4):
                    turn = (lz - 16 * r + 256) & 127
                    y = line_of(ly + 8 * h + r)
                    for b in range(BANDS):
                        for q in range(2):
                            v = jnp.where(group == r, packed[b, q], 0.0)
                            at = pl.ds(lx + 16 + 8 * q, 8)
                            v = turned[b, y, at, :] + pltpu.roll(v, turn, 1)
                            batch.append((b, y, at, v))
                for b, y, at, v in batch:
                    turned[b, y, at, :] = v

        return 0

    if cut:
        number = chosen(starts, counts, lambda live, whole: live & jnp.logical_not(whole), listed)
    else:
        number = chosen(starts, counts, lambda live, whole: live & whole, listed)
    lax.fori_loop(0, number, atom, 0)


def fold(b, i, h, turned):
    flat = turned.reshape(BANDS * (CY + 1) * 48, 128)
    return flat[pl.ds((b * (CY + 1) + 8 * h) * 48 + 16 + i, 8, stride=48), :]


def whole_kernel(
    starts_in, counts_in, coupling_in, proj, sums, acc, out, turned, coef,
    starts, counts, coupling, listed, sems,
):
    tables = (starts, counts, coupling)
    copies = begin(list(zip((starts_in, counts_in, coupling_in), tables)), sems)
    spread(False, copies, tables, listed, proj, sums, turned, coef)
    for b in range(BANDS):
        for i in range(CX):
            for h in range(2):
                at = slice(8 * h, 8 * h + 8)
                out[b, i, at, :] = acc[b, i, at, :] + fold(b, i, h, turned)


def cut_kernel(
    starts_in, counts_in, coupling_in, proj, sums, z_low, z_high, acc, out, turned, coef,
    starts, counts, coupling, listed, sems,
):
    tables = (starts, counts, coupling)
    copies = begin(list(zip((starts_in, counts_in, coupling_in), tables)), sems)
    edge = jnp.concatenate([z_low[...], z_high[...]], axis=0)
    row, lane = iota((16, 128), 0), iota((16, 128), 1)
    far = jnp.where(row < 8, lane + 6 - row, 128 + (row - 8) - lane)
    real = (row & 7) < 6
    tail = jnp.zeros((16, 128), F32)
    for k in range(1, 7):
        tail = jnp.where(real & (far == k), HALF[k], tail)
    z_part = contract(edge, tail, ((0,), (0,))).reshape(BANDS, CX, CY, CZ)
    out[...] = acc[...] + z_part
    spread(True, copies, tables, listed, proj, sums, turned, coef)
    for b in range(BANDS):
        for i in range(CX):
            for h in range(2):
                at = slice(8 * h, 8 * h + 8)
                out[b, i, at, :] = out[b, i, at, :] + fold(b, i, h, turned)


def shape(*dims):
    return jax.ShapeDtypeStruct(dims, F32)


def shifted(value, axis, distance):
    n = lax.axis_size(axis)
    return lax.ppermute(value, axis, [(i, (i + distance) % n) for i in range(n)])


def swapped(value, axis, first):
    n = lax.axis_size(axis)
    pairs = [((first + i) % n, (first + (i ^ 1)) % n) for i in range(n)]
    return lax.ppermute(value, axis, pairs)


def call(kernel, outs, ins, scratch, name, args, flops, bytes_accessed):
    return pl.pallas_call(
        kernel,
        out_shape=outs,
        in_specs=ins,
        out_specs=[VM] * len(outs),
        scratch_shapes=[pltpu.VMEM(s, F32) if isinstance(s, tuple) else s for s in scratch],
        compiler_params=params(),
        cost_estimate=pl.CostEstimate(
            flops=flops, bytes_accessed=bytes_accessed, transcendentals=0
        ),
        name=name,
    )(*args)


def on_device(orbitals, potential, projectors, coupling, block_starts, owner_counts):
    grid = shape(BANDS, CX, CY, CZ)
    padded = (BANDS, CY + 1, 48, 128)
    projectors = projectors.reshape(8, SLOTS, NPROJ, 32, 128).transpose(0, 1, 3, 2, 4)
    projectors = projectors.reshape(8 * SLOTS, 32 * NPROJ, 128)
    starts = block_starts.transpose(0, 1, 2, 5, 4, 3)
    matrices = coupling.transpose(0, 1, 2, 4, 5, 6, 3)

    same, turned, up_x, dn_x, up_y, dn_y = call(
        turn_kernel,
        [grid, shape(*padded)] + [shape(EDGE, 128)] * 4,
        [VM],
        [],
        "turn",
        (orbitals,),
        1 << 30,
        1 << 24,
    )
    (part,) = call(
        gather_kernel,
        [shape(16, 128)],
        [HB, HB, VM, VM],
        [(64, 128), (256, 128)] + PLACES + LISTED,
        "gather",
        (starts, owner_counts, turned, projectors),
        1 << 30,
        1 << 24,
    )

    from_low = shifted(jnp.concatenate([up_x, part[:8]], axis=0), "gx", 1)
    from_high = shifted(jnp.concatenate([dn_x, part[8:]], axis=0), "gx", -1)
    acc, up_z, dn_z = call(
        local_kernel,
        [grid, shape(8, 512), shape(8, 512)],
        [VM] * 2,
        [],
        "local",
        (same, potential),
        1 << 26,
        1 << 20,
    )
    part, acc = lax.optimization_barrier((part, acc))
    x_low, x_high = from_low[:EDGE], from_high[:EDGE]
    sums = part + jnp.concatenate([from_high[EDGE:], from_low[EDGE:]], axis=0)

    from_low = shifted(jnp.concatenate([up_y, sums], axis=0), "gy", 1)
    from_high = shifted(jnp.concatenate([dn_y, sums], axis=0), "gy", -1)
    (acc,) = call(
        x_kernel, [grid], [VM] * 4, [], "along_x", (same, x_low, x_high, acc), 1 << 22, 1 << 20
    )
    sums, acc = lax.optimization_barrier((sums, acc))
    y_low, y_high = from_low[:EDGE], from_high[:EDGE]
    first = (iota((16, 128), 1) & 64) == 0
    sums = sums + jnp.where(
        first, jnp.roll(from_high[EDGE:], -64, 1), jnp.roll(from_low[EDGE:], 64, 1)
    )

    flat = sums.reshape(2, 8, 128).transpose(1, 0, 2).reshape(8, 256)
    odd = lax.rem(lax.axis_index("gz"), 2) == 1
    near = jnp.concatenate([jnp.where(odd, dn_z, up_z), flat], axis=1)
    far = jnp.concatenate([jnp.where(odd, up_z, dn_z), flat], axis=1)
    near = swapped(near, "gz", 0)
    (acc,) = call(
        y_kernel,
        [grid],
        [VM] * 4,
        [(BANDS, CX, 32, 128)],
        "along_y",
        (same, y_low, y_high, acc),
        1 << 22,
        1 << 20,
    )
    far, acc = lax.optimization_barrier((far, acc))
    far = swapped(far, "gz", 1)
    from_high = jnp.where(odd, far, near)
    from_low = jnp.where(odd, near, far)
    (acc,) = call(
        whole_kernel,
        [grid],
        [HB, HB, HB] + [VM] * 3,
        [padded, (256, 128)] + PLACES + MATRICES + LISTED,
        "whole_blocks",
        (starts, owner_counts, matrices, projectors, sums, acc),
        1 << 30,
        1 << 24,
    )
    first = (iota((8, 256), 1) & 32) == 0
    flat = flat + jnp.where(
        first, jnp.roll(from_high[:, 512:], -32, 1), jnp.roll(from_low[:, 512:], 32, 1)
    )
    sums = flat.reshape(8, 2, 128).transpose(1, 0, 2).reshape(16, 128)
    (out,) = call(
        cut_kernel,
        [grid],
        [HB, HB, HB] + [VM] * 5,
        [padded, (256, 128)] + PLACES + MATRICES + LISTED,
        "cut_blocks",
        (
            starts,
            owner_counts,
            matrices,
            projectors,
            sums,
            from_low[:, :512],
            from_high[:, :512],
            acc,
        ),
        1 << 22,
        1 << 20,
    )
    return out


def solution(mesh):
    in_specs = (
        P(None, "gx", "gy", "gz"),
        P("gx", "gy", "gz"),
        P("gx", "gy", "gz", None, None, None, None),
        P("gx", "gy", "gz", None, None, None, None),
        P("gx", "gy", "gz", None, None, None),
        P("gx", "gy", "gz", None),
    )
    out_specs = P(None, "gx", "gy", "gz")
    return jax.shard_map(
        on_device, mesh=mesh, in_specs=in_specs, out_specs=out_specs, check_vma=False
    )
```

```python
import jax
import jax.numpy as jnp
from jax import lax
from jax.experimental import pallas as pl
from jax.experimental.pallas import tpu as pltpu
from jax.sharding import PartitionSpec as P

PB = 16
NPROJ = 4
SLOTS = 4
BANDS = 2
CX = 16
CY = 16
CZ = 128
RADIUS = 6
EDGE = BANDS * RADIUS * CX
MiB = 1 << 20

COEFF = [
    -5369.0 / 1800.0,
    12.0 / 7.0,
    -15.0 / 56.0,
    10.0 / 189.0,
    -1.0 / 112.0,
    2.0 / 1925.0,
    -1.0 / 16632.0,
]
HALF = [-0.5 * c for c in COEFF]
HI = lax.Precision.HIGHEST
F32 = jnp.float32

VM = pl.BlockSpec(memory_space=pltpu.VMEM)
HB = pl.BlockSpec(memory_space=pl.ANY)
PLACES = [
    pltpu.SMEM((1, 1, 1, 3, SLOTS, 8), jnp.int32),
    pltpu.SMEM((1, 1, 1, 8), jnp.int32),
]
MATRICES = [pltpu.SMEM((1, 1, 1, SLOTS, NPROJ, NPROJ, 8), F32)]
LISTED = [pltpu.SMEM((8 * SLOTS,), jnp.int32), pltpu.SemaphoreType.DMA((3,))]


def params():
    return pltpu.CompilerParams(vmem_limit_bytes=24 * MiB)


def iota(shape, dim):
    return lax.broadcasted_iota(jnp.int32, shape, dim)


def contract(a, b, dims):
    return lax.dot_general(a, b, (dims, ((), ())), precision=HI, preferred_element_type=F32)


def place(starts, counts, k):
    o = k >> 2
    s = k & 3
    lx = starts[0, 0, 0, 0, s, o] - CX * (o >> 2)
    ly = starts[0, 0, 0, 1, s, o] - CY * ((o >> 1) & 1)
    lz = starts[0, 0, 0, 2, s, o] - CZ * (o & 1)
    live = (s < counts[0, 0, 0, o]) & (lx > -PB) & (ly > -PB) & (lz > -PB)
    whole = (lz >= 0) & (lz <= CZ - PB)
    return lx, ly, lz, live, whole


def begin(pairs, sems):
    copies = [pltpu.make_async_copy(a, b, sems.at[n]) for n, (a, b) in enumerate(pairs)]
    for copy in copies:
        copy.start()
    return copies


def chosen(starts, counts, which, listed):
    n = jnp.int32(0)
    for k in range(8 * SLOTS):
        _, _, _, live, whole = place(starts, counts, k)
        listed[n] = k
        n = n + which(live, whole).astype(jnp.int32)
    return n


def line_of(y):
    return jnp.where((y >= 0) & (y < CY), y, CY)


def splat(row):
    return jnp.broadcast_to(row, (8, 128))


def turn_about(source, target):
    flat = source.reshape(BANDS * CX * CY, 128)
    zero = jnp.zeros((16, 128), F32)
    for b in range(BANDS):
        for y in range(CY):
            target[b, y, 0:16, :] = zero
            target[b, y, 32:48, :] = zero
            for h in range(2):
                target[b, y, 16 + 8 * h : 24 + 8 * h, :] = flat[
                    pl.ds(256 * b + 128 * h + y, 8, stride=16), :
                ]
        target[b, CY, :, :] = jnp.zeros((48, 128), F32)


def turn_kernel(x, same, turned, up_x, dn_x, up_y, dn_y):
    same[...] = x[...]
    turn_about(x, turned)
    for b in range(BANDS):
        up_x[96 * b : 96 * b + 96, :] = x[b, 10:16].reshape(96, 128)
        dn_x[96 * b : 96 * b + 96, :] = x[b, 0:6].reshape(96, 128)
        for i in range(CX):
            at = (b * CX + i) * RADIUS
            up_y[at : at + RADIUS, :] = x[b, i, 10:16, :]
            dn_y[at : at + RADIUS, :] = x[b, i, 0:6, :]


def gather_kernel(
    starts_in, counts_in, turned, proj, part, sums, rows, starts, counts, listed, sems
):
    copies = begin([(starts_in, starts), (counts_in, counts)], sems)
    rows[...] = jnp.zeros_like(rows)
    for copy in copies:
        copy.wait()
    group = iota((8, 128), 1) >> 4
    cell = iota((8, 128), 1) & 15

    def atom(n, _):
        k = listed[n]
        lx, ly, lz, _, _ = place(starts, counts, k)
        inside = (cell + lz >= 0) & (cell + lz < CZ)
        acc = [None] * 8
        for h in range(2):
            packed = {}
            for r in range(8):
                turn = (16 * r - lz + 128) & 127
                y = line_of(ly + 8 * h + r)
                for b in range(BANDS):
                    for q in range(2):
                        v = turned[b, y, pl.ds(lx + 16 + 8 * q, 8), :]
                        v = pltpu.roll(v, turn, 1)
                        packed[b, q] = v if r == 0 else jnp.where(group == r, v, packed[b, q])
            for q in range(2):
                cells = [jnp.where(inside, packed[b, q], 0.0) for b in range(BANDS)]
                for j in range(NPROJ):
                    p = proj[k, pl.ds(64 * q + 4 * h + j, 8, stride=8), :]
                    for b in range(BANDS):
                        m = b * NPROJ + j
                        t = cells[b] * p
                        acc[m] = t if acc[m] is None else acc[m] + t
        for m in range(8):
            sums[8 * m : 8 * m + 8, :] = acc[m]
        total = sums[pl.ds(0, 8, stride=8), :]
        for m in range(1, 8):
            total = total + sums[pl.ds(m, 8, stride=8), :]
        rows[pl.ds(pl.multiple_of(k * 8, 8), 8), :] = total

        return 0

    number = chosen(starts, counts, lambda live, whole: live, listed)
    lax.fori_loop(0, number, atom, 0)
    coef = contract(jnp.ones((8, 128), F32), rows[...], ((1,), (1,)))
    part[0:8, :] = coef[:, 0:128]
    part[8:16, :] = coef[:, 128:256]


def local_kernel(x, pot, out, up_z, dn_z):
    row, lane = iota((128, 128), 0), iota((128, 128), 1)
    near = jnp.abs(row - lane)
    band = jnp.where(near == 0, 3.0 * HALF[0], 0.0)
    for k in range(1, 7):
        band = jnp.where(near == k, HALF[k], band)
    flat = x[...].reshape(BANDS * CX * CY, 128)
    total = contract(flat, band.astype(F32), ((1,), (0,)))
    out[...] = total.reshape(BANDS, CX, CY, CZ)
    for b in range(BANDS):
        out[b] = out[b] + pot[...] * x[b]
    row, lane = iota((16, 128), 0), iota((16, 128), 1)
    pick_up = (row < 6) & (lane == row + 122)
    pick_dn = (row >= 8) & (row < 14) & (lane == row - 8)
    pick = jnp.where(pick_up | pick_dn, 1.0, 0.0).astype(F32)
    faces = contract(pick, flat, ((1,), (1,)))
    up_z[...] = faces[0:8]
    dn_z[...] = faces[8:16]


def x_kernel(x, low, high, acc, out):
    for b in range(BANDS):

        def plane(i, b=b):
            if i < 0:
                at = 96 * b + 16 * (i + 6)
                return low[at : at + 16, :]
            if i >= CX:
                at = 96 * b + 16 * (i - CX)
                return high[at : at + 16, :]
            return x[b, i]

        for i in range(CX):
            total = acc[b, i]
            for k in range(1, 7):
                total = total + HALF[k] * (plane(i + k) + plane(i - k))
            out[b, i] = total


def y_kernel(x, low, high, acc, out, wide):
    for b in range(BANDS):
        for i in range(CX):
            at = (b * CX + i) * RADIUS
            wide[b, i, 2:8, :] = low[at : at + RADIUS, :]
            wide[b, i, 8:24, :] = x[b, i]
            wide[b, i, 24:30, :] = high[at : at + RADIUS, :]

    for b in range(BANDS):

        def line(i, _, b=b):
            total = acc[b, i]
            for k in range(1, 7):
                total = total + HALF[k] * (
                    wide[b, i, 8 + k : 24 + k, :] + wide[b, i, 8 - k : 24 - k, :]
                )
            out[b, i] = total
            return 0

        lax.fori_loop(0, CX, line, 0, unroll=4)


def spread(cut, copies, tables, listed, proj, sums, turned, coef):
    starts, counts, coupling = tables
    eye = iota((128, 128), 0) == iota((128, 128), 1)
    ones = jnp.ones((128, 128), F32)
    for a in range(2):
        row = jnp.broadcast_to(sums[8 * a : 8 * a + 1, :], (128, 128))
        coef[128 * a : 128 * a + 128, :] = contract(jnp.where(eye, row, 0.0), ones, ((1,), (0,)))
    turned[...] = jnp.zeros_like(turned)
    group = iota((8, 128), 1) >> 4
    cell = iota((8, 128), 1) & 15

    for copy in copies:
        copy.wait()

    def atom(n, _):
        k = listed[n]
        lx, ly, lz, _, _ = place(starts, counts, k)
        inside = (cell + lz >= 0) & (cell + lz < CZ)
        own = coef[pl.ds(pl.multiple_of(k * 8, 8), 8), :]
        weight = []
        for b in range(BANDS):
            c = [splat(own[b * NPROJ + j : b * NPROJ + j + 1, :]) for j in range(NPROJ)]
            for i in range(NPROJ):
                total = coupling[0, 0, 0, k & 3, i, 0, k >> 2] * c[0]
                for j in range(1, NPROJ):
                    total = total + coupling[0, 0, 0, k & 3, i, j, k >> 2] * c[j]
                weight.append(total)
        for h in range(2):
            packed = {}
            for q in range(2):
                p = [
                    proj[k, pl.ds(64 * q + 4 * h + j, 8, stride=8), :] for j in range(NPROJ)
                ]
                for b in range(BANDS):
                    v = weight[b * NPROJ] * p[0]
                    for j in range(1, NPROJ):
                        v = v + weight[b * NPROJ + j] * p[j]
                    packed[b, q] = jnp.where(inside, v, 0.0)
            for half in range(2):
                batch = []
                for r in range(4 * half, 4 * half + 4):
                    turn = (lz - 16 * r + 256) & 127
                    y = line_of(ly + 8 * h + r)
                    for b in range(BANDS):
                        for q in range(2):
                            v = jnp.where(group == r, packed[b, q], 0.0)
                            at = pl.ds(lx + 16 + 8 * q, 8)
                            v = turned[b, y, at, :] + pltpu.roll(v, turn, 1)
                            batch.append((b, y, at, v))
                for b, y, at, v in batch:
                    turned[b, y, at, :] = v

        return 0

    if cut:
        number = chosen(starts, counts, lambda live, whole: live & jnp.logical_not(whole), listed)
    else:
        number = chosen(starts, counts, lambda live, whole: live & whole, listed)
    lax.fori_loop(0, number, atom, 0)


def fold(b, i, h, turned):
    flat = turned.reshape(BANDS * (CY + 1) * 48, 128)
    return flat[pl.ds((b * (CY + 1) + 8 * h) * 48 + 16 + i, 8, stride=48), :]


def whole_kernel(
    starts_in, counts_in, coupling_in, proj, sums, acc, out, turned, coef,
    starts, counts, coupling, listed, sems,
):
    tables = (starts, counts, coupling)
    copies = begin(list(zip((starts_in, counts_in, coupling_in), tables)), sems)
    spread(False, copies, tables, listed, proj, sums, turned, coef)
    for b in range(BANDS):
        for i in range(CX):
            for h in range(2):
                at = slice(8 * h, 8 * h + 8)
                out[b, i, at, :] = acc[b, i, at, :] + fold(b, i, h, turned)


def cut_kernel(
    starts_in, counts_in, coupling_in, proj, sums, z_low, z_high, acc, result, turned, coef,
    starts, counts, coupling, listed, sems, out, sent,
):
    tables = (starts, counts, coupling)
    copies = begin(list(zip((starts_in, counts_in, coupling_in), tables)), sems)
    edge = jnp.concatenate([z_low[...], z_high[...]], axis=0)
    row, lane = iota((16, 128), 0), iota((16, 128), 1)
    far = jnp.where(row < 8, lane + 6 - row, 128 + (row - 8) - lane)
    real = (row & 7) < 6
    tail = jnp.zeros((16, 128), F32)
    for k in range(1, 7):
        tail = jnp.where(real & (far == k), HALF[k], tail)
    z_part = contract(edge, tail, ((0,), (0,))).reshape(BANDS, CX, CY, CZ)
    out[...] = acc[...] + z_part
    spread(True, copies, tables, listed, proj, sums, turned, coef)
    leaving = []
    for b in range(BANDS):
        for i in range(CX):
            for h in range(2):
                at = slice(8 * h, 8 * h + 8)
                out[b, i, at, :] = out[b, i, at, :] + fold(b, i, h, turned)
            if i % 8 == 7:
                planes = pl.ds(i - 7, 8)
                copy = pltpu.make_async_copy(
                    out.at[b, planes], result.at[b, planes], sent.at[2 * b + i // 8]
                )
                copy.start()
                leaving.append(copy)
    for copy in leaving:
        copy.wait()


def shape(*dims):
    return jax.ShapeDtypeStruct(dims, F32)


def shifted(value, axis, distance):
    n = lax.axis_size(axis)
    return lax.ppermute(value, axis, [(i, (i + distance) % n) for i in range(n)])


def swapped(value, axis, first):
    n = lax.axis_size(axis)
    pairs = [((first + i) % n, (first + (i ^ 1)) % n) for i in range(n)]
    return lax.ppermute(value, axis, pairs)


def call(kernel, outs, ins, scratch, name, args, flops, bytes_accessed, place_of=VM):
    return pl.pallas_call(
        kernel,
        out_shape=outs,
        in_specs=ins,
        out_specs=[place_of] * len(outs),
        scratch_shapes=[pltpu.VMEM(s, F32) if isinstance(s, tuple) else s for s in scratch],
        compiler_params=params(),
        cost_estimate=pl.CostEstimate(
            flops=flops, bytes_accessed=bytes_accessed, transcendentals=0
        ),
        name=name,
    )(*args)


def on_device(orbitals, potential, projectors, coupling, block_starts, owner_counts):
    grid = shape(BANDS, CX, CY, CZ)
    padded = (BANDS, CY + 1, 48, 128)
    projectors = projectors.reshape(8, SLOTS, NPROJ, 32, 128).transpose(0, 1, 3, 2, 4)
    projectors = projectors.reshape(8 * SLOTS, 32 * NPROJ, 128)
    starts = block_starts.transpose(0, 1, 2, 5, 4, 3)
    matrices = coupling.transpose(0, 1, 2, 4, 5, 6, 3)

    same, turned, up_x, dn_x, up_y, dn_y = call(
        turn_kernel,
        [grid, shape(*padded)] + [shape(EDGE, 128)] * 4,
        [VM],
        [],
        "turn",
        (orbitals,),
        1 << 30,
        1 << 24,
    )
    (part,) = call(
        gather_kernel,
        [shape(16, 128)],
        [HB, HB, VM, VM],
        [(64, 128), (256, 128)] + PLACES + LISTED,
        "gather",
        (starts, owner_counts, turned, projectors),
        1 << 30,
        1 << 24,
    )

    from_low = shifted(jnp.concatenate([up_x, part[:8]], axis=0), "gx", 1)
    from_high = shifted(jnp.concatenate([dn_x, part[8:]], axis=0), "gx", -1)
    acc, up_z, dn_z = call(
        local_kernel,
        [grid, shape(8, 512), shape(8, 512)],
        [VM] * 2,
        [],
        "local",
        (same, potential),
        1 << 26,
        1 << 20,
    )
    part, acc = lax.optimization_barrier((part, acc))
    x_low, x_high = from_low[:EDGE], from_high[:EDGE]
    sums = part + jnp.concatenate([from_high[EDGE:], from_low[EDGE:]], axis=0)

    from_low = shifted(jnp.concatenate([up_y, sums], axis=0), "gy", 1)
    from_high = shifted(jnp.concatenate([dn_y, sums], axis=0), "gy", -1)
    (acc,) = call(
        x_kernel, [grid], [VM] * 4, [], "along_x", (same, x_low, x_high, acc), 1 << 22, 1 << 20
    )
    sums, acc = lax.optimization_barrier((sums, acc))
    y_low, y_high = from_low[:EDGE], from_high[:EDGE]
    first = (iota((16, 128), 1) & 64) == 0
    sums = sums + jnp.where(
        first, jnp.roll(from_high[EDGE:], -64, 1), jnp.roll(from_low[EDGE:], 64, 1)
    )

    flat = sums.reshape(2, 8, 128).transpose(1, 0, 2).reshape(8, 256)
    odd = lax.rem(lax.axis_index("gz"), 2) == 1
    near = jnp.concatenate([jnp.where(odd, dn_z, up_z), flat], axis=1)
    far = jnp.concatenate([jnp.where(odd, up_z, dn_z), flat], axis=1)
    near = swapped(near, "gz", 0)
    (acc,) = call(
        y_kernel,
        [grid],
        [VM] * 4,
        [(BANDS, CX, 32, 128)],
        "along_y",
        (same, y_low, y_high, acc),
        1 << 22,
        1 << 20,
    )
    far, acc = lax.optimization_barrier((far, acc))
    far = swapped(far, "gz", 1)
    from_high = jnp.where(odd, far, near)
    from_low = jnp.where(odd, near, far)
    (acc,) = call(
        whole_kernel,
        [grid],
        [HB, HB, HB] + [VM] * 3,
        [padded, (256, 128)] + PLACES + MATRICES + LISTED,
        "whole_blocks",
        (starts, owner_counts, matrices, projectors, sums, acc),
        1 << 30,
        1 << 24,
    )
    first = (iota((8, 256), 1) & 32) == 0
    flat = flat + jnp.where(
        first, jnp.roll(from_high[:, 512:], -32, 1), jnp.roll(from_low[:, 512:], 32, 1)
    )
    sums = flat.reshape(8, 2, 128).transpose(1, 0, 2).reshape(16, 128)
    (out,) = call(
        cut_kernel,
        [grid],
        [HB, HB, HB] + [VM] * 5,
        [padded, (256, 128)]
        + PLACES
        + MATRICES
        + LISTED
        + [(BANDS, CX, CY, CZ), pltpu.SemaphoreType.DMA((4,))],
        "cut_blocks",
        (
            starts,
            owner_counts,
            matrices,
            projectors,
            sums,
            from_low[:, :512],
            from_high[:, :512],
            acc,
        ),
        1 << 22,
        1 << 20,
        HB,
    )
    return out


def solution(mesh):
    in_specs = (
        P(None, "gx", "gy", "gz"),
        P("gx", "gy", "gz"),
        P("gx", "gy", "gz", None, None, None, None),
        P("gx", "gy", "gz", None, None, None, None),
        P("gx", "gy", "gz", None, None, None),
        P("gx", "gy", "gz", None),
    )
    out_specs = P(None, "gx", "gy", "gz")
    return jax.shard_map(
        on_device, mesh=mesh, in_specs=in_specs, out_specs=out_specs, check_vma=False
    )
```
